128 devices in a mesh: blk: 8 (over x_lo, z), grp: 16 (over y, x_hi, core).
Axes of the slice: x: 4 (x_hi: 2, x_lo: 2; x = x_hi * 2 + x_lo), y: 4, z: 4, core: 2. Of those that a mesh axis runs over, the one named last changes fastest.
Arguments:
- global_desc: bfloat16 [65536, 1024], P(('grp', 'blk')), may hold values from -0.1875 to 0.1875
- key_points: bfloat16 [512, 512, 256], P(('grp', 'blk')), may hold values from -1 to 1
- pair_first: int32 [1536], P(('grp', 'blk')), may hold values from 0 to 3
- pair_second: int32 [1536], P(('grp', 'blk')), may hold values from 0 to 63, as said below
Outputs:
- expanded: bfloat16 [65536, 1024], P(('grp', 'blk'))
- confidence: float32 [1536, 2, 512], P(('grp', 'blk'))
The draws below stay inside these ranges and needn't reach their ends.
Inputs may be any that keep to these rules, and one draw needn't show every extreme that they name: pair_second[p] = g * 4 + r names image r of the device at grp index g and the owner's blk index. Among one device's 12 pairs at most 2 name images of one source device, and every device has a source with exactly 2.
All inputs are finite; a program needn't handle non-finite values.
Results may differ from the reference program's by a relative error of at most 0.0029.
Values may be sent and summed in bfloat16 or wider, within the bound.
No kernel may reach another device: no remote copies, remote signals or barrier semaphores. Data moves between devices by JAX's collectives and lax.ppermute only.
A program may use at most 128 MiB of HBM per device.

```python
import math
import jax
import jax.numpy as jnp
from jax import lax

DG = 1024
DK = 256
K = 512
IMG_DEV = 512
KP_DEV = 4
PAIRS_DEV = 12
CAP = 2
IMAGES = 65536
PAIRS = 1536
N_BLK = 8
N_GRP = 16


def draw_key_points(key, part):
    key = jax.random.fold_in(key, 7)
    key_base = jax.random.fold_in(key, 0)
    count = KP_DEV * N_GRP * N_BLK
    scale = 0.32 * DK ** (-0.25)
    values = jnp.clip(scale * jax.random.normal(key_base, (count, K, DK), jnp.float32), -6.0 * scale, 6.0 * scale)
    return values.astype(jnp.bfloat16)


def draw_pair_second(key, part):
    key = jax.random.fold_in(key, 5)
    devices = N_GRP * N_BLK

    def one_device(device_key):
        key_busy, key_rest, key_order, key_rows = jax.random.split(device_key, 4)
        busiest = jax.random.randint(key_busy, (), 0, N_GRP)
        others = (busiest + 1 + jnp.arange((N_GRP - 1) * CAP) // CAP) % N_GRP
        others = jax.random.permutation(key_rest, others)[:PAIRS_DEV - CAP]
        sources = jnp.concatenate([jnp.full((CAP,), busiest, jnp.int32), others.astype(jnp.int32)])
        sources = jax.random.permutation(key_order, sources)
        rows = jax.random.randint(key_rows, (PAIRS_DEV,), 0, KP_DEV)
        return (sources * KP_DEV + rows).astype(jnp.int32)
    device_keys = jax.random.split(key, devices)
    return jax.vmap(one_device)(device_keys).reshape(-1).astype(jnp.int32)


def plant(array, rng, smallest, high):
    dims = array.shape
    place = [jax.random.randint(jax.random.fold_in(rng, axis), (), 0, dims[axis]) for axis in range(len(dims))]
    array = array.at[tuple(place)].set(smallest)
    longest = dims.index(max(dims))
    place[longest] = (place[longest] + 1) % dims[longest]
    return array.at[tuple(place)].set(high)


def level_of(key, extent, cuts, least, high):
    gain, own = 1.0, jax.random.fold_in(key, 6)
    for position, blocks in cuts:
        steps = jnp.exp(jax.random.uniform(jax.random.fold_in(own, position), (blocks,), jnp.float32, least / len(cuts), high / len(cuts)))
        gain = gain * jnp.repeat(steps, extent[position] // blocks).reshape([-1 if axis == position else 1 for axis in range(len(extent))])
    return gain


def gaussian(key, extent, width, bound, pieces=(), kind=jnp.bfloat16):
    result = width * jax.random.normal(key, extent, jnp.float32)
    if pieces:
        result = result * level_of(key, extent, pieces, -0.22, 0.18)
    return jnp.clip(result, -bound, bound).astype(kind)


def setup_inputs(seed: int = 0) -> dict:
    keys = jax.random.split(jax.random.key(seed), 5)
    global_desc = gaussian(keys[0], (IMAGES, DG), DG ** -0.5, 0.1875, ((0, 128),))
    key_points = draw_key_points(jax.random.fold_in(keys[4], 71), 0)
    pair_first = plant(jax.random.randint(keys[2], (PAIRS,), 0, KP_DEV), jax.random.fold_in(keys[2], 1), 0, KP_DEV - 1).astype(jnp.int32)
    pair_second = draw_pair_second(jax.random.fold_in(keys[4], 71), 0)
    return dict(global_desc=global_desc, key_points=key_points, pair_first=pair_first, pair_second=pair_second)


softmax_sharpness = 10.0
epsilon = 1e-06

def expand_group(members):
    whole = members.reshape(N_BLK * IMG_DEV, DG)

    def one_block(rows):
        sims = jnp.dot(rows, whole.T, preferred_element_type=jnp.float32)
        weights = jnp.maximum(sims, 0.0).astype(jnp.bfloat16)
        totals = jnp.dot(weights, whole, preferred_element_type=jnp.float32)
        scale = lax.rsqrt(lax.optimization_barrier(jnp.mean(totals * totals, axis=1, keepdims=True)) + epsilon)
        return (totals * scale).astype(jnp.bfloat16)
    return lax.map(one_block, members)

def reference(global_desc, key_points, pair_first, pair_second):
    groups = global_desc.reshape(N_GRP, N_BLK, IMG_DEV, DG)
    expanded = lax.map(expand_group, groups).reshape(IMAGES, DG)
    owner = (jnp.arange(PAIRS) // PAIRS_DEV).astype(jnp.int32)
    column = owner % N_BLK
    first = (owner * KP_DEV + pair_first).astype(jnp.int32)
    second = ((pair_second // KP_DEV * N_BLK + column) * KP_DEV + pair_second % KP_DEV).astype(jnp.int32)
    indices = jnp.stack([first, second], axis=1)

    def one_pair(index_pair):
        pair_source_image = key_points[index_pair[0]].astype(jnp.float32)
        pair_target_image = key_points[index_pair[1]].astype(jnp.float32)
        similarity_scores = jnp.dot(pair_source_image, pair_target_image.T, precision=lax.Precision.HIGHEST) * softmax_sharpness
        row_sum_exponent = jax.nn.logsumexp(similarity_scores, axis=1)
        col_total = jax.nn.logsumexp(similarity_scores, axis=0)
        match_log_probability = 2.0 * similarity_scores - row_sum_exponent[:, None] - col_total[None, :] + 2.0 * math.log(K)
        return jnp.stack([lax.optimization_barrier(jnp.max(match_log_probability, axis=1)), lax.optimization_barrier(jnp.max(match_log_probability, axis=0))], axis=0)
    confidence = lax.map(one_pair, indices)
    return (expanded, confidence)
```

```python
import functools
import math

import jax
import jax.numpy as jnp
from jax import lax
from jax.experimental import pallas as pl
from jax.experimental.pallas import tpu as pltpu
from jax.sharding import PartitionSpec as P

softmax_sharpness = 10.0
epsilon = 1e-06
log2_e = 1.4426950408889634

Z_UP = [(x * 4 + z, x * 4 + (z + 1) % 4) for x in range(2) for z in range(4)]
Z_DOWN = [(b, a) for a, b in Z_UP]
X_PAIR = [(i, i ^ 4) for i in range(8)]
Y_UP = [(y * 4 + k, (y + 1) % 4 * 4 + k) for y in range(4) for k in range(4)]
Y_DOWN = [(b, a) for a, b in Y_UP]
CORE = [(i, i ^ 1) for i in range(16)]
X_FAR = [(i, i ^ 2) for i in range(16)]
X_FAR_CORE = [(i, i ^ 3) for i in range(16)]


def fold_lanes(op, x):
    return op(op(x[:, 0:128], x[:, 128:256]), op(x[:, 256:384], x[:, 384:512]))


def match_pair(a_ref, b_ref, t_ref, lse_ref, out_ref, where):
    n, m = t_ref.shape
    rows = 128
    half = 0.5 / softmax_sharpness
    offset = 2.0 * math.log(m)
    col = jnp.zeros((8, m), jnp.float32)
    row_sums = []
    for k in range(n // rows):
        sl = slice(k * rows, (k + 1) * rows)
        t = lax.dot_general(
            a_ref[sl, :], b_ref[...], (((1,), (1,)), ((), ())), preferred_element_type=jnp.float32
        )
        t_ref[sl, :] = t
        e = jnp.exp2(t * (softmax_sharpness * log2_e))
        row_sums.append(jnp.sum(jnp.transpose(fold_lanes(jnp.add, e)), axis=0, keepdims=True))
        col = col + jnp.sum(e.reshape(rows // 8, 8, m), axis=0)
    col_sum = jnp.sum(col, axis=0, keepdims=True)
    row_sum = jnp.concatenate(row_sums, axis=1)
    low = jnp.min(jnp.minimum(col_sum, row_sum))
    high = jnp.max(jnp.maximum(col_sum, row_sum))
    in_range = (low > 1e-25) & (high < 1e30)
    lse_ref[0:1, :] = jnp.log(col_sum)
    lse_ref[1:2, :] = jnp.log(row_sum)

    @pl.when(jnp.logical_not(in_range))
    def _():
        s = t_ref[...] * softmax_sharpness
        peak = jnp.max(s, axis=0, keepdims=True)
        lse_ref[0:1, :] = jnp.log(jnp.sum(jnp.exp(s - peak), axis=0, keepdims=True)) + peak
        peak = jnp.max(s, axis=1, keepdims=True)
        row = jnp.log(jnp.sum(jnp.exp(s - peak), axis=1, keepdims=True)) + peak
        lse_ref[1:2, :] = jnp.transpose(jnp.broadcast_to(row, (n, 128)))[0:1, :]

    c = lse_ref[0:1, :]
    r = lse_ref[1:2, :]
    c_half = c * half
    r_half = r * half
    best = jnp.full((8, m), -jnp.inf, jnp.float32)
    row_best = []
    for k in range(n // rows):
        sl = slice(k * rows, (k + 1) * rows)
        t = t_ref[sl, :]
        r_tile = jnp.transpose(jnp.broadcast_to(r_half[:, sl], (128, rows)))
        r_tile = jnp.concatenate([r_tile] * (m // 128), axis=1)
        best = jnp.maximum(best, jnp.max((t - r_tile).reshape(rows // 8, 8, m), axis=0))
        row_best.append(
            jnp.max(jnp.transpose(fold_lanes(jnp.maximum, t - c_half)), axis=0, keepdims=True)
        )
    out_ref[where, 0:1, :] = jnp.concatenate(row_best, axis=1) * (1.0 / half) - r + offset
    out_ref[where, 1:2, :] = jnp.max(best, axis=0, keepdims=True) * (1.0 / half) - c + offset


def pairs_kernel(
    place_ref, meta_ref, f0, f1, f2, f3, s0, s1, s2a, s2b, s3,
    out_ref, list_ref, a_buf, b_buf, t_ref, lse_ref, sems,
):
    owners, _, count = meta_ref.shape
    mine = place_ref[0]
    my_y = place_ref[1]

    def collect(i, n):
        owner = i // count
        p = i - owner * count
        second = meta_ref[owner, 1, p]
        source = second // 4
        hit = source % 4 == mine

        @pl.when(hit)
        def _():
            list_ref[0, n] = owner
            list_ref[1, n] = meta_ref[owner, 0, p]
            list_ref[2, n] = (source // 4 - my_y + 4) % 4
            list_ref[3, n] = second % 4
            list_ref[4, n] = i

        return n + hit.astype(jnp.int32)

    total = lax.fori_loop(0, owners * count, collect, 0)

    def fetch(i, slot):
        owner, first = list_ref[0, i], list_ref[1, i]
        step, row = list_ref[2, i], list_ref[3, i]
        for k, ref in enumerate((f0, f1, f2, f3)):
            @pl.when(owner == k)
            def _():
                pltpu.make_async_copy(ref.at[first], a_buf.at[slot], sems.at[0, slot]).start()
        for k, ref in ((0, s0), (1, s1), (3, s3)):
            @pl.when(step == k)
            def _():
                pltpu.make_async_copy(ref.at[row], b_buf.at[slot], sems.at[1, slot]).start()

        @pl.when((step == 2) & (row < 2))
        def _():
            pltpu.make_async_copy(s2a.at[row], b_buf.at[slot], sems.at[1, slot]).start()

        @pl.when((step == 2) & (row >= 2))
        def _():
            pltpu.make_async_copy(s2b.at[row - 2], b_buf.at[slot], sems.at[1, slot]).start()

    @pl.when(total > 0)
    def _():
        fetch(0, 0)

    def one(i, carry):
        slot = lax.rem(i, 2)

        @pl.when(i + 1 < total)
        def _():
            fetch(i + 1, 1 - slot)

        pltpu.make_async_copy(f0.at[0], a_buf.at[slot], sems.at[0, slot]).wait()
        pltpu.make_async_copy(s0.at[0], b_buf.at[slot], sems.at[1, slot]).wait()
        match_pair(a_buf.at[slot], b_buf.at[slot], t_ref, lse_ref, out_ref, list_ref[4, i])
        return carry

    lax.fori_loop(0, total, one, 0)


def match_pairs(place, meta, firsts, seconds):
    owners, _, count = meta.shape
    _, n, width = firsts[0].shape
    smem = pl.BlockSpec(memory_space=pltpu.SMEM)
    hbm = pl.BlockSpec(memory_space=pl.ANY)
    return pl.pallas_call(
        pairs_kernel,
        out_shape=jax.ShapeDtypeStruct((owners * count, 2, n), jnp.float32),
        in_specs=[smem, smem] + [hbm] * 9,
        out_specs=pl.BlockSpec(memory_space=pltpu.VMEM),
        scratch_shapes=[
            pltpu.SMEM((5, owners * count), jnp.int32),
            pltpu.VMEM((2, n, width), jnp.bfloat16),
            pltpu.VMEM((2, n, width), jnp.bfloat16),
            pltpu.VMEM((n, n), jnp.float32),
            pltpu.VMEM((8, n), jnp.float32),
            pltpu.SemaphoreType.DMA((2, 2)),
        ],
        compiler_params=pltpu.CompilerParams(vmem_limit_bytes=16 * 2**20),
        cost_estimate=pl.CostEstimate(
            flops=12 * 2 * n * n * width, bytes_accessed=12 * 4 * n * width, transcendentals=12 * n * n
        ),
        name="match_pairs",
    )(place, meta, *firsts, *seconds)


def after(x, *deps):
    return lax.optimization_barrier((x,) + deps)[0]


def add_piece(total, rows, piece):
    sims = lax.dot_general(
        rows, piece, (((1,), (1,)), ((), ())), preferred_element_type=jnp.float32
    )
    weights = jnp.maximum(sims, 0.0).astype(jnp.bfloat16)
    part = jnp.dot(weights, piece, preferred_element_type=jnp.float32)
    return part if total is None else total + part


def on_device(global_desc, key_points, pair_first, pair_second):
    g = lax.axis_index("grp")
    half = global_desc.shape[0] // 2

    up, down = (lambda v: lax.ppermute(v, "blk", Z_UP)), (lambda v: lax.ppermute(v, "blk", Z_DOWN))
    own = global_desc
    own_up = up(own)
    own_down = down(own)
    pair = lax.ppermute(own, "blk", X_PAIR)
    k_up = lax.ppermute(key_points, "grp", Y_UP)
    k_down = lax.ppermute(key_points, "grp", Y_DOWN)
    meta = jnp.stack([pair_first, pair_second])
    meta = jnp.stack([meta, lax.ppermute(meta, "grp", CORE)])
    meta = jnp.concatenate([meta, lax.ppermute(meta, "grp", X_FAR)])
    k_core = lax.ppermute(key_points, "grp", CORE)
    k_far = lax.ppermute(after(key_points, pair), "grp", X_FAR)
    k_far_core = lax.ppermute(k_far, "grp", CORE)
    k_two_a = lax.ppermute(k_up[:2], "grp", Y_UP)
    k_two_b = lax.ppermute(k_down[2:], "grp", Y_DOWN)

    own_two_a = up(own_up[:half])
    own_two_b = down(own_down[half:])
    pair_up = up(pair)
    pair_down = down(pair)
    pair_two_a = up(pair_up[:half])
    pair_two_b = down(pair_down[half:])

    place = jnp.stack([g % 4, g // 4])
    found = match_pairs(
        place, meta, (key_points, k_core, k_far, k_far_core),
        (key_points, k_down, k_two_a, k_two_b, k_up),
    )
    count = pair_second.shape[0]
    found = found.reshape(4, count, 2, key_points.shape[1])
    back = [
        found[0],
        lax.ppermute(found[1], "grp", CORE),
        lax.ppermute(found[2], "grp", X_FAR),
        lax.ppermute(found[3], "grp", X_FAR_CORE),
    ]
    handler = ((pair_second // 4) % 4 ^ (g % 4))[:, None, None]
    confidence = jnp.where(
        handler == 0, back[0], jnp.where(handler == 1, back[1], jnp.where(handler == 2, back[2], back[3]))
    )

    total = add_piece(None, own, own)
    for piece in (own_up, own_down, pair, own_two_a, own_two_b, pair_up, pair_down, pair_two_a, pair_two_b):
        total = add_piece(total, own, piece)
    scale = lax.rsqrt(jnp.mean(total * total, axis=1, keepdims=True) + epsilon)
    expanded = (total * scale).astype(jnp.bfloat16)
    return (expanded, confidence)


def solution(mesh):
    in_specs = (
        P(("grp", "blk"), None),
        P(("grp", "blk"), None, None),
        P(("grp", "blk")),
        P(("grp", "blk")),
    )
    out_specs = (P(("grp", "blk"), None), P(("grp", "blk"), None, None))
    return jax.shard_map(
        on_device, mesh=mesh, in_specs=in_specs, out_specs=out_specs, check_vma=False
    )
```

```python
import functools
import math

import jax
import jax.numpy as jnp
from jax import lax
from jax.experimental import pallas as pl
from jax.experimental.pallas import tpu as pltpu
from jax.sharding import PartitionSpec as P

softmax_sharpness = 10.0
epsilon = 1e-06
log2_e = 1.4426950408889634
vmem_bytes = 12 * 2**20

def steps(axis, turn):
    pairs = []
    for device in range(128):
        blk, grp = device // 16, device % 16
        hop = turn if grp % 2 == 0 else -turn
        if axis == "z":
            blk = blk // 4 * 4 + (blk + hop) % 4
        else:
            grp = (grp // 4 + hop) % 4 * 4 + grp % 4
        pairs.append((device, blk * 16 + grp))
    return pairs


BOTH = ("blk", "grp")
Z_1, Z_2, Y_1, Y_2 = steps("z", 1), steps("z", -1), steps("y", 1), steps("y", -1)
X_PAIR = [(i, i ^ 4) for i in range(8)]
CORE = [(i, i ^ 1) for i in range(16)]
X_FAR = [(i, i ^ 2) for i in range(16)]
X_FAR_CORE = [(i, i ^ 3) for i in range(16)]


def fold_lanes(op, x):
    return op(op(x[:, 0:128], x[:, 128:256]), op(x[:, 256:384], x[:, 384:512]))


def confidences(t, row_lse, col_lse, out_ref, where):
    rows, m = t[0].shape
    half = 0.5 / softmax_sharpness
    offset = 2.0 * math.log(m)
    row_half, col_half = row_lse * half, col_lse * half
    best = jnp.full((8, m), -jnp.inf, jnp.float32)
    row_best = []
    for k, part in enumerate(t):
        part = part[...]
        sl = slice(k * rows, (k + 1) * rows)
        tile = jnp.transpose(jnp.broadcast_to(row_half[:, sl], (128, rows)))
        tile = jnp.concatenate([tile] * (m // 128), axis=1)
        best = jnp.maximum(best, jnp.max((part - tile).reshape(rows // 8, 8, m), axis=0))
        row_best.append(
            jnp.max(jnp.transpose(fold_lanes(jnp.maximum, part - col_half)), axis=0, keepdims=True)
        )
    out_ref[where, 0:1, :] = jnp.concatenate(row_best, axis=1) * (1.0 / half) - row_lse + offset
    out_ref[where, 1:2, :] = jnp.max(best, axis=0, keepdims=True) * (1.0 / half) - col_lse + offset


def match_two(pairs, out_ref):
    rows = 256
    sums = []
    for a_ref, b_ref, t_ref, _ in pairs:
        n, m = t_ref.shape
        col = jnp.zeros((8, m), jnp.float32)
        row_sums = []
        for k in range(n // rows):
            sl = slice(k * rows, (k + 1) * rows)
            t = lax.dot_general(
                a_ref[sl, :], b_ref[...], (((1,), (1,)), ((), ())), preferred_element_type=jnp.float32
            )
            t_ref[sl, :] = t
            e = jnp.exp2(t * (softmax_sharpness * log2_e))
            row_sums.append(jnp.sum(jnp.transpose(fold_lanes(jnp.add, e)), axis=0, keepdims=True))
            col = col + jnp.sum(e.reshape(rows // 8, 8, m), axis=0)
        sums.append((jnp.concatenate(row_sums, axis=1), jnp.sum(col, axis=0, keepdims=True)))
    low = functools.reduce(jnp.minimum, [x for both in sums for x in both])
    high = functools.reduce(jnp.maximum, [x for both in sums for x in both])
    in_range = (jnp.min(low) > 1e-25) & (jnp.max(high) < 1e30)
    for (_, _, t_ref, where), (row_sum, col_sum) in zip(pairs, sums):
        parts = [t_ref.at[k:k + rows, :] for k in range(0, t_ref.shape[0], rows)]
        confidences(parts, jnp.log(row_sum), jnp.log(col_sum), out_ref, where)

    @pl.when(jnp.logical_not(in_range))
    def _():
        for _, _, t_ref, where in pairs:
            n = t_ref.shape[0]
            s = t_ref[...] * softmax_sharpness
            peak = jnp.max(s, axis=0, keepdims=True)
            col_lse = jnp.log(jnp.sum(jnp.exp(s - peak), axis=0, keepdims=True)) + peak
            peak = jnp.max(s, axis=1, keepdims=True)
            row_lse = jnp.log(jnp.sum(jnp.exp(s - peak), axis=1, keepdims=True)) + peak
            row_lse = jnp.transpose(jnp.broadcast_to(row_lse, (n, 128)))[0:1, :]
            parts = [t_ref.at[k:k + rows, :] for k in range(0, n, rows)]
            confidences(parts, row_lse, col_lse, out_ref, where)


def pairs_kernel(place_ref, meta_ref, *rest, owners, steps, skip):
    rest = list(rest)
    firsts = [rest.pop(0) for _ in range(owners)]
    seconds = {step: rest.pop(0) for step in steps}
    before_ref = rest.pop(0) if skip else None
    out_ref, list_ref, a_0, b_0, t_0, a_1, b_1, t_1 = rest
    lists, _, count = meta_ref.shape
    n = t_0.shape[0]
    mine, my_y = place_ref[0], place_ref[1]
    turn = 1 + 2 * place_ref[2]
    if skip:
        out_ref[...] = before_ref[...]

    total = jnp.int32(0)
    for owner in range(lists):
        for p in range(count):
            second = meta_ref[owner, 1, p]
            source = lax.shift_right_logical(second, 2)
            step = ((lax.shift_right_logical(source, 2) - my_y + 4) * turn) & 3
            hit = (source & 3) == mine
            if skip:
                done_owners, done_steps = skip
                if owner < done_owners:
                    hit = hit & functools.reduce(
                        jnp.logical_and, [step != k for k in done_steps]
                    )
            elif len(steps) < 4:
                hit = hit & functools.reduce(jnp.logical_or, [step == k for k in steps])
            list_ref[total] = (
                (owner + (owner * count + p) * 256) + meta_ref[owner, 0, p] * 4 + step * 16 + (second & 3) * 64
            )
            total = total + hit.astype(jnp.int32)

    def load(i, a_ref, b_ref):
        code = list_ref[jnp.minimum(i, total - 1)]
        owner = code & 3
        image = lax.shift_right_logical(code, 2) & 3
        step = lax.shift_right_logical(code, 4) & 3
        row = lax.shift_right_logical(code, 6) & 3
        rows = pl.ds(pl.multiple_of(image * n, n), n)
        for k, ref in enumerate(firsts[:3]):
            @pl.when(owner == k)
            def _():
                a_ref[...] = ref[image] if len(ref.shape) == 3 else ref[rows, :]
        for k, ref in enumerate(firsts[3:]):
            @pl.when((owner == 3) & (image == k))
            def _():
                a_ref[...] = ref[...]
        for k, ref in seconds.items():
            @pl.when(step == k)
            def _():
                b_ref[...] = ref[row]
        return lax.shift_right_logical(code, 8)

    def two(i, carry):
        where_0 = load(2 * i, a_0, b_0)
        where_1 = load(2 * i + 1, a_1, b_1)
        match_two(((a_0, b_0, t_0, where_0), (a_1, b_1, t_1, where_1)), out_ref)
        return carry

    lax.fori_loop(0, lax.shift_right_logical(total + 1, 1), two, 0)


def match_pairs(place, meta, firsts, seconds, before=None, skip=None):
    _, n, width = seconds[0].shape
    count = meta.shape[2]
    smem = pl.BlockSpec(memory_space=pltpu.SMEM)
    vmem = pl.BlockSpec(memory_space=pltpu.VMEM)
    arrays = (*firsts, *seconds.values()) + (() if before is None else (before,))
    return pl.pallas_call(
        functools.partial(pairs_kernel, owners=len(firsts), steps=tuple(seconds), skip=skip),
        out_shape=jax.ShapeDtypeStruct((4 * count, 2, n), jnp.float32),
        in_specs=[smem, smem] + [vmem] * len(arrays),
        out_specs=vmem,
        scratch_shapes=[
            pltpu.SMEM((4 * count + 1,), jnp.int32),
        ] + 2 * [
            pltpu.VMEM((n, width), jnp.bfloat16),
            pltpu.VMEM((n, width), jnp.bfloat16),
            pltpu.VMEM((n, n), jnp.float32),
        ],
        compiler_params=pltpu.CompilerParams(vmem_limit_bytes=vmem_bytes),
        cost_estimate=pl.CostEstimate(
            flops=n, bytes_accessed=n, transcendentals=0
        ),
        name="match_pairs",
    )(place, meta, *arrays)


def after(x, *deps):
    return lax.optimization_barrier((x,) + deps)[0]


def block_kernel(own_ref, *rest, pieces, first, last):
    rest = list(rest)
    blocks = [rest.pop(0) for _ in range(pieces)]
    total_ref = None if first else rest.pop(0)
    out_ref, weights_ref = rest[:2]
    wide = 256
    n = own_ref.shape[1]
    at = 0
    for block in blocks:
        for q in range(0, block.shape[0], wide):
            sims = lax.dot_general(
                own_ref[...], block[q:q + wide, :], (((1,), (1,)), ((), ())),
                preferred_element_type=jnp.float32,
            )
            weights_ref[:, at:at + wide] = jnp.maximum(sims, 0.0).astype(jnp.bfloat16)
            at += wide
    square = None
    for c in range(0, n, wide):
        total = None if first else total_ref[:, c:c + wide]
        at = 0
        for block in blocks:
            h = block.shape[0]
            part = jnp.dot(
                weights_ref[:, at:at + h], block[:, c:c + wide], preferred_element_type=jnp.float32
            )
            total = part if total is None else total + part
            at += h
        if last:
            total_ref[:, c:c + wide] = total
            folded = total[:, :128] * total[:, :128] + total[:, 128:] * total[:, 128:]
            square = folded if square is None else square + folded
        else:
            out_ref[:, c:c + wide] = total
    if last:
        scale = lax.rsqrt(jnp.sum(square, axis=1, keepdims=True) * (1.0 / n) + epsilon)
        for c in range(0, n, wide):
            out_ref[:, c:c + wide] = (total_ref[:, c:c + wide] * scale).astype(out_ref.dtype)


def add_blocks(own, blocks, total=None, last=False):
    rows, n = own.shape
    count = sum(b.shape[0] for b in blocks)
    vmem = pl.BlockSpec(memory_space=pltpu.VMEM)
    args = (own, *blocks) + (() if total is None else (total,))
    return pl.pallas_call(
        functools.partial(block_kernel, pieces=len(blocks), first=total is None, last=last),
        out_shape=jax.ShapeDtypeStruct((rows, n), jnp.bfloat16 if last else jnp.float32),
        in_specs=[vmem] * len(args),
        out_specs=vmem,
        scratch_shapes=[pltpu.VMEM((rows, count), jnp.bfloat16)],
        compiler_params=pltpu.CompilerParams(vmem_limit_bytes=vmem_bytes),
        cost_estimate=pl.CostEstimate(
            flops=n, bytes_accessed=n, transcendentals=0
        ),
        name="add_blocks",
    )(*args)


def join_kernel(a_ref, b_ref, out_ref):
    out_ref[: a_ref.shape[0], :] = a_ref[...]
    out_ref[a_ref.shape[0]:, :] = b_ref[...]


def join(a, b):
    vmem = pl.BlockSpec(memory_space=pltpu.VMEM)
    return pl.pallas_call(
        join_kernel,
        out_shape=jax.ShapeDtypeStruct((a.shape[0] + b.shape[0], a.shape[1]), a.dtype),
        in_specs=[vmem] * 2,
        out_specs=vmem,
        compiler_params=pltpu.CompilerParams(vmem_limit_bytes=vmem_bytes),
        cost_estimate=pl.CostEstimate(flops=1, bytes_accessed=1, transcendentals=0),
        name="join",
    )(a, b)


def split_kernel(a_ref, *rest):
    outs, sems = rest[:-1], rest[-1]
    rows = outs[0].shape[0]
    copies = [
        pltpu.make_async_copy(a_ref.at[i * rows:(i + 1) * rows], out, sems.at[i])
        for i, out in enumerate(outs)
    ]
    for copy in copies:
        copy.start()
    for copy in copies:
        copy.wait()


def split(a, count):
    hbm = pl.BlockSpec(memory_space=pl.ANY)
    rows, width = a.shape[0] // count // 16 * 16, a.shape[1]
    return pl.pallas_call(
        split_kernel,
        out_shape=[jax.ShapeDtypeStruct((rows, width), a.dtype)] * count,
        in_specs=[hbm],
        out_specs=[hbm] * count,
        scratch_shapes=[pltpu.SemaphoreType.DMA((count,))],
        compiler_params=pltpu.CompilerParams(vmem_limit_bytes=vmem_bytes),
        cost_estimate=pl.CostEstimate(flops=1, bytes_accessed=1, transcendentals=0),
        name="split",
    )(a)


def on_device(global_desc, key_points, pair_first, pair_second):
    g = lax.axis_index("grp")
    images, n, width = key_points.shape
    count = pair_second.shape[0]

    def move(v, perm):
        return lax.ppermute(v, BOTH, perm)

    own = global_desc
    own_1 = move(own, Z_1)
    own_2 = move(own, Z_2)
    pair = lax.ppermute(own, "blk", X_PAIR)
    k_core = lax.ppermute(key_points, "grp", CORE)
    k_1 = move(key_points, Y_1)
    lists = jnp.stack([pair_first, pair_second])
    near = jnp.stack([lists, lax.ppermute(lists, "grp", CORE)])
    rows = near.reshape(4, count).astype(jnp.bfloat16)
    rows = jnp.zeros((16, width), jnp.bfloat16).at[:4, :count].set(rows)
    sheet = jnp.concatenate([key_points.reshape(images * n, width), rows])
    own_1, own_2, pair, sheet, near = lax.optimization_barrier((own_1, own_2, pair, sheet, near))

    pair_1 = move(pair, Z_1)
    own_3_pair_2 = move(join(own_2, pair), Z_2)
    k_3 = move(after(k_1, pair), Y_1)
    k_2 = move(after(key_points, pair, k_core), Y_2)
    sheet_far = lax.ppermute(sheet, "grp", X_FAR)
    total = add_blocks(own, (own, own_1, own_2, pair))
    place = jnp.stack([g % 4, g // 4, g % 2])
    found = match_pairs(place, after(near, total), (key_points, k_core), {0: key_points, 1: k_2, 3: k_1})


    pair_3 = move(after(pair_1, found, k_3), Z_1)
    total = add_blocks(own, (pair_1,), total)
    far_core = [lax.ppermute(v, "grp", CORE) for v in split(after(sheet_far, found, total), images)]
    far = sheet_far[images * n:images * n + 4, :count].astype(jnp.int32).reshape(2, 2, count)
    every = jnp.concatenate([near, far])
    found = match_pairs(
        place, every, (key_points, k_core, sheet_far, *far_core),
        {0: key_points, 1: k_2, 2: k_3, 3: k_1}, found, (2, (0, 1, 3)),
    )
    found = found.reshape(4, count, 2, n)
    back = [
        found[0],
        lax.ppermute(found[1], "grp", CORE),
        lax.ppermute(found[2], "grp", X_FAR),
        lax.ppermute(found[3], "grp", X_FAR_CORE),
    ]
    total = add_blocks(own, (own_3_pair_2,), after(total, found))
    expanded = add_blocks(own, (pair_3,), total, last=True)
    handler = (pair_second // 4) % 4 ^ (g % 4)
    handler = after(handler, expanded)[:, None, None]
    confidence = jnp.where(
        handler == 0, back[0], jnp.where(handler == 1, back[1], jnp.where(handler == 2, back[2], back[3]))
    )
    return (expanded, confidence)


def solution(mesh):
    in_specs = (
        P(("grp", "blk"), None),
        P(("grp", "blk"), None, None),
        P(("grp", "blk")),
        P(("grp", "blk")),
    )
    out_specs = (P(("grp", "blk"), None), P(("grp", "blk"), None, None))
    return jax.shard_map(
        on_device, mesh=mesh, in_specs=in_specs, out_specs=out_specs, check_vma=False
    )
```

```python
import functools
import math

import jax
import jax.numpy as jnp
from jax import lax
from jax.experimental import pallas as pl
from jax.experimental.pallas import tpu as pltpu
from jax.sharding import PartitionSpec as P

softmax_sharpness = 10.0
epsilon = 1e-06
log2_e = 1.4426950408889634
vmem_bytes = 12 * 2**20

def steps(axis, turn):
    pairs = []
    for device in range(128):
        blk, grp = device // 16, device % 16
        hop = turn if grp % 2 == 0 else -turn
        if axis == "z":
            blk = blk // 4 * 4 + (blk + hop) % 4
        else:
            grp = (grp // 4 + hop) % 4 * 4 + grp % 4
        pairs.append((device, blk * 16 + grp))
    return pairs


BOTH = ("blk", "grp")
Z_1, Z_2, Y_1, Y_2 = steps("z", 1), steps("z", -1), steps("y", 1), steps("y", -1)
X_PAIR = [(i, i ^ 4) for i in range(8)]
CORE = [(i, i ^ 1) for i in range(16)]
X_FAR = [(i, i ^ 2) for i in range(16)]
X_FAR_CORE = [(i, i ^ 3) for i in range(16)]


def fold_lanes(op, x):
    return op(op(x[:, 0:128], x[:, 128:256]), op(x[:, 256:384], x[:, 384:512]))


def confidences(t, row_lse, col_lse, out_ref, where):
    rows, m = t[0].shape
    half = 0.5 / softmax_sharpness
    offset = 2.0 * math.log(m)
    row_half, col_half = row_lse * half, col_lse * half
    best = jnp.full((8, m), -jnp.inf, jnp.float32)
    row_best = []
    for k, part in enumerate(t):
        part = part[...]
        sl = slice(k * rows, (k + 1) * rows)
        tile = jnp.transpose(jnp.broadcast_to(row_half[:, sl], (128, rows)))
        tile = jnp.concatenate([tile] * (m // 128), axis=1)
        best = jnp.maximum(best, jnp.max((part - tile).reshape(rows // 8, 8, m), axis=0))
        row_best.append(
            jnp.max(jnp.transpose(fold_lanes(jnp.maximum, part - col_half)), axis=0, keepdims=True)
        )
    out_ref[where, 0:1, :] = jnp.concatenate(row_best, axis=1) * (1.0 / half) - row_lse + offset
    out_ref[where, 1:2, :] = jnp.max(best, axis=0, keepdims=True) * (1.0 / half) - col_lse + offset


def match_two(pairs, out_ref):
    rows = 256
    sums = []
    for a_ref, b_ref, t_ref, _ in pairs:
        n, m = t_ref.shape
        col = jnp.zeros((8, m), jnp.float32)
        row_sums = []
        for k in range(n // rows):
            sl = slice(k * rows, (k + 1) * rows)
            t = lax.dot_general(
                a_ref[sl, :], b_ref[...], (((1,), (1,)), ((), ())), preferred_element_type=jnp.float32
            )
            t_ref[sl, :] = t
            e = jnp.exp2(t * (softmax_sharpness * log2_e))
            row_sums.append(jnp.sum(jnp.transpose(fold_lanes(jnp.add, e)), axis=0, keepdims=True))
            col = col + jnp.sum(e.reshape(rows // 8, 8, m), axis=0)
        sums.append((jnp.concatenate(row_sums, axis=1), jnp.sum(col, axis=0, keepdims=True)))
    low = functools.reduce(jnp.minimum, [x for both in sums for x in both])
    high = functools.reduce(jnp.maximum, [x for both in sums for x in both])
    in_range = (jnp.min(low) > 1e-25) & (jnp.max(high) < 1e30)
    for (_, _, t_ref, where), (row_sum, col_sum) in zip(pairs, sums):
        parts = [t_ref.at[k:k + rows, :] for k in range(0, t_ref.shape[0], rows)]
        confidences(parts, jnp.log(row_sum), jnp.log(col_sum), out_ref, where)

    @pl.when(jnp.logical_not(in_range))
    def _():
        for _, _, t_ref, where in pairs:
            n = t_ref.shape[0]
            s = t_ref[...] * softmax_sharpness
            peak = jnp.max(s, axis=0, keepdims=True)
            col_lse = jnp.log(jnp.sum(jnp.exp(s - peak), axis=0, keepdims=True)) + peak
            peak = jnp.max(s, axis=1, keepdims=True)
            row_lse = jnp.log(jnp.sum(jnp.exp(s - peak), axis=1, keepdims=True)) + peak
            row_lse = jnp.transpose(jnp.broadcast_to(row_lse, (n, 128)))[0:1, :]
            parts = [t_ref.at[k:k + rows, :] for k in range(0, n, rows)]
            confidences(parts, row_lse, col_lse, out_ref, where)


def pairs_kernel(place_ref, meta_ref, *rest, owners, steps, skip):
    rest = list(rest)
    firsts = [rest.pop(0) for _ in range(owners)]
    seconds = {step: rest.pop(0) for step in steps}
    before_ref = rest.pop(0) if skip else None
    out_ref, list_ref, a_0, b_0, t_0, a_1, b_1, t_1 = rest
    lists, _, count = meta_ref.shape
    n = t_0.shape[0]
    mine, my_y = place_ref[0], place_ref[1]
    turn = 1 + 2 * place_ref[2]
    if skip:
        out_ref[...] = before_ref[...]

    total = jnp.int32(0)
    for owner in range(lists):
        for p in range(count):
            second = meta_ref[owner, 1, p]
            source = lax.shift_right_logical(second, 2)
            step = ((lax.shift_right_logical(source, 2) - my_y + 4) * turn) & 3
            hit = (source & 3) == mine
            if skip:
                done_owners, done_steps = skip
                if owner < done_owners:
                    hit = hit & functools.reduce(
                        jnp.logical_and, [step != k for k in done_steps]
                    )
            elif len(steps) < 4:
                hit = hit & functools.reduce(jnp.logical_or, [step == k for k in steps])
            list_ref[total] = (
                (owner + (owner * count + p) * 256) + meta_ref[owner, 0, p] * 4 + step * 16 + (second & 3) * 64
            )
            total = total + hit.astype(jnp.int32)

    def load(i, a_ref, b_ref):
        code = list_ref[jnp.minimum(i, total - 1)]
        owner = code & 3
        image = lax.shift_right_logical(code, 2) & 3
        step = lax.shift_right_logical(code, 4) & 3
        row = lax.shift_right_logical(code, 6) & 3
        rows = pl.ds(pl.multiple_of(image * n, n), n)
        for k, ref in enumerate(firsts[:3]):
            @pl.when(owner == k)
            def _():
                a_ref[...] = ref[image] if len(ref.shape) == 3 else ref[rows, :]
        for k, ref in enumerate(firsts[3:]):
            held = ref.shape[0] // n
            @pl.when((owner == 3) & (image >= k * held) & (image < (k + 1) * held))
            def _():
                inside = pl.multiple_of((image - k * held) * n, n)
                a_ref[...] = ref[pl.ds(inside, n), :]
        for k, ref in seconds.items():
            @pl.when(step == k)
            def _():
                b_ref[...] = ref[row]
        return lax.shift_right_logical(code, 8)

    def two(i, carry):
        where_0 = load(2 * i, a_0, b_0)
        where_1 = load(2 * i + 1, a_1, b_1)
        match_two(((a_0, b_0, t_0, where_0), (a_1, b_1, t_1, where_1)), out_ref)
        return carry

    lax.fori_loop(0, lax.shift_right_logical(total + 1, 1), two, 0)


def match_pairs(place, meta, firsts, seconds, before=None, skip=None):
    _, n, width = seconds[0].shape
    count = meta.shape[2]
    smem = pl.BlockSpec(memory_space=pltpu.SMEM)
    vmem = pl.BlockSpec(memory_space=pltpu.VMEM)
    arrays = (*firsts, *seconds.values()) + (() if before is None else (before,))
    return pl.pallas_call(
        functools.partial(pairs_kernel, owners=len(firsts), steps=tuple(seconds), skip=skip),
        out_shape=jax.ShapeDtypeStruct((4 * count, 2, n), jnp.float32),
        in_specs=[smem, smem] + [vmem] * len(arrays),
        out_specs=vmem,
        scratch_shapes=[
            pltpu.SMEM((4 * count + 1,), jnp.int32),
        ] + 2 * [
            pltpu.VMEM((n, width), jnp.bfloat16),
            pltpu.VMEM((n, width), jnp.bfloat16),
            pltpu.VMEM((n, n), jnp.float32),
        ],
        compiler_params=pltpu.CompilerParams(vmem_limit_bytes=vmem_bytes),
        cost_estimate=pl.CostEstimate(
            flops=n, bytes_accessed=n, transcendentals=0
        ),
        name="match_pairs",
    )(place, meta, *arrays)


def after(x, *deps):
    return lax.optimization_barrier((x,) + deps)[0]


def block_kernel(own_ref, *rest, pieces, first, last):
    rest = list(rest)
    blocks = [rest.pop(0) for _ in range(pieces)]
    total_ref = None if first else rest.pop(0)
    out_ref, weights_ref = rest[:2]
    wide = 256
    n = own_ref.shape[1]
    at = 0
    for block in blocks:
        for q in range(0, block.shape[0], wide):
            sims = lax.dot_general(
                own_ref[...], block[q:q + wide, :], (((1,), (1,)), ((), ())),
                preferred_element_type=jnp.float32,
            )
            weights_ref[:, at:at + wide] = jnp.maximum(sims, 0.0).astype(jnp.bfloat16)
            at += wide
    square = None
    for c in range(0, n, wide):
        total = None if first else total_ref[:, c:c + wide]
        at = 0
        for block in blocks:
            h = block.shape[0]
            part = jnp.dot(
                weights_ref[:, at:at + h], block[:, c:c + wide], preferred_element_type=jnp.float32
            )
            total = part if total is None else total + part
            at += h
        if last:
            total_ref[:, c:c + wide] = total
            folded = total[:, :128] * total[:, :128] + total[:, 128:] * total[:, 128:]
            square = folded if square is None else square + folded
        else:
            out_ref[:, c:c + wide] = total
    if last:
        scale = lax.rsqrt(jnp.sum(square, axis=1, keepdims=True) * (1.0 / n) + epsilon)
        for c in range(0, n, wide):
            out_ref[:, c:c + wide] = (total_ref[:, c:c + wide] * scale).astype(out_ref.dtype)


def add_blocks(own, blocks, total=None, last=False):
    rows, n = own.shape
    count = sum(b.shape[0] for b in blocks)
    vmem = pl.BlockSpec(memory_space=pltpu.VMEM)
    args = (own, *blocks) + (() if total is None else (total,))
    return pl.pallas_call(
        functools.partial(block_kernel, pieces=len(blocks), first=total is None, last=last),
        out_shape=jax.ShapeDtypeStruct((rows, n), jnp.bfloat16 if last else jnp.float32),
        in_specs=[vmem] * len(args),
        out_specs=vmem,
        scratch_shapes=[pltpu.VMEM((rows, count), jnp.bfloat16)],
        compiler_params=pltpu.CompilerParams(vmem_limit_bytes=vmem_bytes),
        cost_estimate=pl.CostEstimate(
            flops=n, bytes_accessed=n, transcendentals=0
        ),
        name="add_blocks",
    )(*args)


def join_kernel(a_ref, b_ref, out_ref):
    out_ref[: a_ref.shape[0], :] = a_ref[...]
    out_ref[a_ref.shape[0]:, :] = b_ref[...]


def join(a, b):
    vmem = pl.BlockSpec(memory_space=pltpu.VMEM)
    return pl.pallas_call(
        join_kernel,
        out_shape=jax.ShapeDtypeStruct((a.shape[0] + b.shape[0], a.shape[1]), a.dtype),
        in_specs=[vmem] * 2,
        out_specs=vmem,
        compiler_params=pltpu.CompilerParams(vmem_limit_bytes=vmem_bytes),
        cost_estimate=pl.CostEstimate(flops=1, bytes_accessed=1, transcendentals=0),
        name="join",
    )(a, b)


def split_kernel(a_ref, *rest):
    outs, sems = rest[:-1], rest[-1]
    rows = outs[0].shape[0]
    copies = [
        pltpu.make_async_copy(a_ref.at[i * rows:(i + 1) * rows], out, sems.at[i])
        for i, out in enumerate(outs)
    ]
    for copy in copies:
        copy.start()
    for copy in copies:
        copy.wait()


def split(a, count):
    hbm = pl.BlockSpec(memory_space=pl.ANY)
    rows, width = a.shape[0] // count // 16 * 16, a.shape[1]
    return pl.pallas_call(
        split_kernel,
        out_shape=[jax.ShapeDtypeStruct((rows, width), a.dtype)] * count,
        in_specs=[hbm],
        out_specs=[hbm] * count,
        scratch_shapes=[pltpu.SemaphoreType.DMA((count,))],
        compiler_params=pltpu.CompilerParams(vmem_limit_bytes=vmem_bytes),
        cost_estimate=pl.CostEstimate(flops=1, bytes_accessed=1, transcendentals=0),
        name="split",
    )(a)


def on_device(global_desc, key_points, pair_first, pair_second):
    g = lax.axis_index("grp")
    images, n, width = key_points.shape
    count = pair_second.shape[0]

    def move(v, perm):
        return lax.ppermute(v, BOTH, perm)

    own = global_desc
    own_1 = move(own, Z_1)
    own_2 = move(own, Z_2)
    pair = lax.ppermute(own, "blk", X_PAIR)
    k_core = lax.ppermute(key_points, "grp", CORE)
    k_1 = move(key_points, Y_1)
    lists = jnp.stack([pair_first, pair_second])
    near = jnp.stack([lists, lax.ppermute(lists, "grp", CORE)])
    rows = near.reshape(4, count).astype(jnp.bfloat16)
    rows = jnp.zeros((16, width), jnp.bfloat16).at[:4, :count].set(rows)
    sheet = jnp.concatenate([key_points.reshape(images * n, width), rows])
    place = jnp.stack([g % 4, g // 4, g % 2])
    handler = (pair_second // 4) % 4 ^ (g % 4)
    own_1, own_2, pair, sheet, near, place, handler = lax.optimization_barrier(
        (own_1, own_2, pair, sheet, near, place, handler)
    )

    pair_1 = move(pair, Z_1)
    own_3_pair_2 = move(join(own_2, pair), Z_2)
    k_3 = move(after(k_1, pair), Y_1)
    k_2 = move(after(key_points, pair, k_core), Y_2)
    sheet_far = lax.ppermute(sheet, "grp", X_FAR)
    total = add_blocks(own, (own, own_1, own_2, pair))
    found = match_pairs(place, after(near, total), (key_points, k_core), {0: key_points, 1: k_2, 3: k_1})


    pair_3 = move(after(pair_1, found, k_3), Z_1)
    total = add_blocks(own, (pair_1,), total)
    far_core = [lax.ppermute(v, "grp", CORE) for v in split(after(sheet_far, found, total), 2)]
    far = sheet_far[images * n:images * n + 4, :count].astype(jnp.int32).reshape(2, 2, count)
    every = jnp.concatenate([near, far])
    found = match_pairs(
        place, every, (key_points, k_core, sheet_far, *far_core),
        {0: key_points, 1: k_2, 2: k_3, 3: k_1}, found, (2, (0, 1, 3)),
    )
    found = found.reshape(4, count, 2, n)
    back = [
        found[0],
        lax.ppermute(found[1], "grp", CORE),
        lax.ppermute(found[2], "grp", X_FAR),
        lax.ppermute(found[3], "grp", X_FAR_CORE),
    ]
    total = add_blocks(own, (own_3_pair_2,), after(total, found))
    expanded = add_blocks(own, (pair_3,), total, last=True)
    handler = after(handler, expanded)[:, None, None]
    confidence = jnp.where(
        handler == 0, back[0], jnp.where(handler == 1, back[1], jnp.where(handler == 2, back[2], back[3]))
    )
    return (expanded, confidence)


def solution(mesh):
    in_specs = (
        P(("grp", "blk"), None),
        P(("grp", "blk"), None, None),
        P(("grp", "blk")),
        P(("grp", "blk")),
    )
    out_specs = (P(("grp", "blk"), None), P(("grp", "blk"), None, None))
    return jax.shard_map(
        on_device, mesh=mesh, in_specs=in_specs, out_specs=out_specs, check_vma=False
    )
```

```python
import functools
import math

import jax
import jax.numpy as jnp
from jax import lax
from jax.experimental import pallas as pl
from jax.experimental.pallas import tpu as pltpu
from jax.sharding import PartitionSpec as P

softmax_sharpness = 10.0
epsilon = 1e-06
log2_e = 1.4426950408889634
vmem_bytes = 12 * 2**20

def steps(axis, turn):
    pairs = []
    for device in range(128):
        blk, grp = device // 16, device % 16
        hop = turn if grp % 2 == 0 else -turn
        if axis == "z":
            blk = blk // 4 * 4 + (blk + hop) % 4
        else:
            grp = (grp // 4 + hop) % 4 * 4 + grp % 4
        pairs.append((device, blk * 16 + grp))
    return pairs


BOTH = ("blk", "grp")
Z_1, Z_2, Y_1, Y_2 = steps("z", 1), steps("z", -1), steps("y", 1), steps("y", -1)
X_PAIR = [(i, i ^ 4) for i in range(8)]
CORE = [(i, i ^ 1) for i in range(16)]
X_FAR = [(i, i ^ 2) for i in range(16)]
X_FAR_CORE = [(i, i ^ 3) for i in range(16)]


def fold_lanes(op, x):
    return op(op(x[:, 0:128], x[:, 128:256]), op(x[:, 256:384], x[:, 384:512]))


def confidences(t, row_lse, col_lse, out_ref, where):
    rows, m = t[0].shape
    half = 0.5 / softmax_sharpness
    offset = 2.0 * math.log(m)
    row_half, col_half = row_lse * half, col_lse * half
    best = jnp.full((8, m), -jnp.inf, jnp.float32)
    row_best = []
    for k, part in enumerate(t):
        part = part[...]
        sl = slice(k * rows, (k + 1) * rows)
        tile = jnp.transpose(jnp.broadcast_to(row_half[:, sl], (128, rows)))
        tile = jnp.concatenate([tile] * (m // 128), axis=1)
        best = jnp.maximum(best, jnp.max((part - tile).reshape(rows // 8, 8, m), axis=0))
        row_best.append(
            jnp.max(jnp.transpose(fold_lanes(jnp.maximum, part - col_half)), axis=0, keepdims=True)
        )
    out_ref[where, 0:1, :] = jnp.concatenate(row_best, axis=1) * (1.0 / half) - row_lse + offset
    out_ref[where, 1:2, :] = jnp.max(best, axis=0, keepdims=True) * (1.0 / half) - col_lse + offset


def match_two(pairs, out_ref):
    rows = 256
    sums = []
    for a_ref, b_ref, t_ref, _ in pairs:
        n, m = t_ref.shape
        col = jnp.zeros((8, m), jnp.float32)
        row_sums = []
        for k in range(n // rows):
            sl = slice(k * rows, (k + 1) * rows)
            t = lax.dot_general(
                a_ref[sl, :], b_ref[...], (((1,), (1,)), ((), ())), preferred_element_type=jnp.float32
            )
            t_ref[sl, :] = t
            e = jnp.exp2(t * (softmax_sharpness * log2_e))
            row_sums.append(jnp.sum(jnp.transpose(fold_lanes(jnp.add, e)), axis=0, keepdims=True))
            col = col + jnp.sum(e.reshape(rows // 8, 8, m), axis=0)
        sums.append((jnp.concatenate(row_sums, axis=1), jnp.sum(col, axis=0, keepdims=True)))
    low = functools.reduce(jnp.minimum, [x for both in sums for x in both])
    high = functools.reduce(jnp.maximum, [x for both in sums for x in both])
    in_range = (jnp.min(low) > 1e-25) & (jnp.max(high) < 1e30)
    for (_, _, t_ref, where), (row_sum, col_sum) in zip(pairs, sums):
        parts = [t_ref.at[k:k + rows, :] for k in range(0, t_ref.shape[0], rows)]
        confidences(parts, jnp.log(row_sum), jnp.log(col_sum), out_ref, where)

    @pl.when(jnp.logical_not(in_range))
    def _():
        for _, _, t_ref, where in pairs:
            n = t_ref.shape[0]
            s = t_ref[...] * softmax_sharpness
            peak = jnp.max(s, axis=0, keepdims=True)
            col_lse = jnp.log(jnp.sum(jnp.exp(s - peak), axis=0, keepdims=True)) + peak
            peak = jnp.max(s, axis=1, keepdims=True)
            row_lse = jnp.log(jnp.sum(jnp.exp(s - peak), axis=1, keepdims=True)) + peak
            row_lse = jnp.transpose(jnp.broadcast_to(row_lse, (n, 128)))[0:1, :]
            parts = [t_ref.at[k:k + rows, :] for k in range(0, n, rows)]
            confidences(parts, row_lse, col_lse, out_ref, where)


def pairs_kernel(place_ref, meta_ref, *rest, owners, steps, skip):
    rest = list(rest)
    firsts = [rest.pop(0) for _ in range(owners)]
    seconds = {step: rest.pop(0) for step in steps}
    before_ref = rest.pop(0) if skip else None
    out_ref, list_ref, a_0, b_0, t_0, a_1, b_1, t_1 = rest
    lists, _, count = meta_ref.shape
    n = t_0.shape[0]
    mine, my_y = place_ref[0], place_ref[1]
    turn = 1 + 2 * place_ref[2]
    if skip:
        out_ref[...] = before_ref[...]

    total = jnp.int32(0)
    for owner in range(lists):
        for p in range(count):
            second = meta_ref[owner, 1, p]
            source = lax.shift_right_logical(second, 2)
            step = ((lax.shift_right_logical(source, 2) - my_y + 4) * turn) & 3
            hit = (source & 3) == mine
            if skip:
                done_owners, done_steps = skip
                if owner < done_owners:
                    hit = hit & functools.reduce(
                        jnp.logical_and, [step != k for k in done_steps]
                    )
            elif len(steps) < 4:
                hit = hit & functools.reduce(jnp.logical_or, [step == k for k in steps])
            list_ref[total] = (
                (owner + (owner * count + p) * 256) + meta_ref[owner, 0, p] * 4 + step * 16 + (second & 3) * 64
            )
            total = total + hit.astype(jnp.int32)

    def load(i, a_ref, b_ref):
        code = list_ref[jnp.minimum(i, total - 1)]
        owner = code & 3
        image = lax.shift_right_logical(code, 2) & 3
        step = lax.shift_right_logical(code, 4) & 3
        row = lax.shift_right_logical(code, 6) & 3
        rows = pl.ds(pl.multiple_of(image * n, n), n)
        for k, ref in enumerate(firsts[:3]):
            @pl.when(owner == k)
            def _():
                a_ref[...] = ref[image] if len(ref.shape) == 3 else ref[rows, :]
        for k, ref in enumerate(firsts[3:]):
            held = ref.shape[0] // n
            @pl.when((owner == 3) & (image >= k * held) & (image < (k + 1) * held))
            def _():
                inside = pl.multiple_of((image - k * held) * n, n)
                a_ref[...] = ref[pl.ds(inside, n), :]
        for k, ref in seconds.items():
            @pl.when(step == k)
            def _():
                b_ref[...] = ref[row]
        return lax.shift_right_logical(code, 8)

    def two(i, carry):
        where_0 = load(2 * i, a_0, b_0)
        where_1 = load(2 * i + 1, a_1, b_1)
        match_two(((a_0, b_0, t_0, where_0), (a_1, b_1, t_1, where_1)), out_ref)
        return carry

    lax.fori_loop(0, lax.shift_right_logical(total + 1, 1), two, 0)


def match_pairs(place, meta, firsts, seconds, before=None, skip=None):
    _, n, width = seconds[3].shape
    count = meta.shape[2]
    smem = pl.BlockSpec(memory_space=pltpu.SMEM)
    vmem = pl.BlockSpec(memory_space=pltpu.VMEM)
    arrays = (*firsts, *seconds.values()) + (() if before is None else (before,))
    return pl.pallas_call(
        functools.partial(pairs_kernel, owners=len(firsts), steps=tuple(seconds), skip=skip),
        out_shape=jax.ShapeDtypeStruct((4 * count, 2, n), jnp.float32),
        in_specs=[smem, smem] + [vmem] * len(arrays),
        out_specs=vmem,
        scratch_shapes=[
            pltpu.SMEM((4 * count + 1,), jnp.int32),
        ] + 2 * [
            pltpu.VMEM((n, width), jnp.bfloat16),
            pltpu.VMEM((n, width), jnp.bfloat16),
            pltpu.VMEM((n, n), jnp.float32),
        ],
        compiler_params=pltpu.CompilerParams(vmem_limit_bytes=vmem_bytes),
        cost_estimate=pl.CostEstimate(
            flops=n, bytes_accessed=n, transcendentals=0
        ),
        name="match_pairs",
    )(place, meta, *arrays)


def after(x, *deps):
    return lax.optimization_barrier((x,) + deps)[0]


def block_kernel(own_ref, *rest, pieces, first, last):
    rest = list(rest)
    blocks = [rest.pop(0) for _ in range(pieces)]
    total_ref = None if first else rest.pop(0)
    out_ref, weights_ref = rest[:2]
    wide = 256
    n = own_ref.shape[1]
    at = 0
    for block in blocks:
        for q in range(0, block.shape[0], wide):
            sims = lax.dot_general(
                own_ref[...], block[q:q + wide, :], (((1,), (1,)), ((), ())),
                preferred_element_type=jnp.float32,
            )
            weights_ref[:, at:at + wide] = jnp.maximum(sims, 0.0).astype(jnp.bfloat16)
            at += wide
    square = None
    for c in range(0, n, wide):
        total = None if first else total_ref[:, c:c + wide]
        at = 0
        for block in blocks:
            h = block.shape[0]
            part = jnp.dot(
                weights_ref[:, at:at + h], block[:, c:c + wide], preferred_element_type=jnp.float32
            )
            total = part if total is None else total + part
            at += h
        if last:
            total_ref[:, c:c + wide] = total
            folded = total[:, :128] * total[:, :128] + total[:, 128:] * total[:, 128:]
            square = folded if square is None else square + folded
        else:
            out_ref[:, c:c + wide] = total
    if last:
        scale = lax.rsqrt(jnp.sum(square, axis=1, keepdims=True) * (1.0 / n) + epsilon)
        for c in range(0, n, wide):
            out_ref[:, c:c + wide] = (total_ref[:, c:c + wide] * scale).astype(out_ref.dtype)


def add_blocks(own, blocks, total=None, last=False):
    rows, n = own.shape
    count = sum(b.shape[0] for b in blocks)
    vmem = pl.BlockSpec(memory_space=pltpu.VMEM)
    args = (own, *blocks) + (() if total is None else (total,))
    return pl.pallas_call(
        functools.partial(block_kernel, pieces=len(blocks), first=total is None, last=last),
        out_shape=jax.ShapeDtypeStruct((rows, n), jnp.bfloat16 if last else jnp.float32),
        in_specs=[vmem] * len(args),
        out_specs=vmem,
        scratch_shapes=[pltpu.VMEM((rows, count), jnp.bfloat16)],
        compiler_params=pltpu.CompilerParams(vmem_limit_bytes=vmem_bytes),
        cost_estimate=pl.CostEstimate(
            flops=n, bytes_accessed=n, transcendentals=0
        ),
        name="add_blocks",
    )(*args)


def join_kernel(a_ref, b_ref, out_ref):
    out_ref[: a_ref.shape[0], :] = a_ref[...]
    out_ref[a_ref.shape[0]:, :] = b_ref[...]


def join(a, b):
    vmem = pl.BlockSpec(memory_space=pltpu.VMEM)
    return pl.pallas_call(
        join_kernel,
        out_shape=jax.ShapeDtypeStruct((a.shape[0] + b.shape[0], a.shape[1]), a.dtype),
        in_specs=[vmem] * 2,
        out_specs=vmem,
        compiler_params=pltpu.CompilerParams(vmem_limit_bytes=vmem_bytes),
        cost_estimate=pl.CostEstimate(flops=1, bytes_accessed=1, transcendentals=0),
        name="join",
    )(a, b)


def split_kernel(a_ref, *rest):
    outs, sems = rest[:-1], rest[-1]
    rows = outs[0].shape[0]
    copies = [
        pltpu.make_async_copy(a_ref.at[i * rows:(i + 1) * rows], out, sems.at[i])
        for i, out in enumerate(outs)
    ]
    for copy in copies:
        copy.start()
    for copy in copies:
        copy.wait()


def split(a, count):
    hbm = pl.BlockSpec(memory_space=pl.ANY)
    rows, width = a.shape[0] // count // 16 * 16, a.shape[1]
    return pl.pallas_call(
        split_kernel,
        out_shape=[jax.ShapeDtypeStruct((rows, width), a.dtype)] * count,
        in_specs=[hbm],
        out_specs=[hbm] * count,
        scratch_shapes=[pltpu.SemaphoreType.DMA((count,))],
        compiler_params=pltpu.CompilerParams(vmem_limit_bytes=vmem_bytes),
        cost_estimate=pl.CostEstimate(flops=1, bytes_accessed=1, transcendentals=0),
        name="split",
    )(a)


def on_device(global_desc, key_points, pair_first, pair_second):
    g = lax.axis_index("grp")
    images, n, width = key_points.shape
    count = pair_second.shape[0]

    def move(v, perm):
        return lax.ppermute(v, BOTH, perm)

    own = global_desc
    own_1 = move(own, Z_1)
    own_2 = move(own, Z_2)
    pair = lax.ppermute(own, "blk", X_PAIR)
    k_core = lax.ppermute(key_points, "grp", CORE)
    k_1 = move(key_points, Y_1)
    lists = jnp.stack([pair_first, pair_second])
    near = jnp.stack([lists, lax.ppermute(lists, "grp", CORE)])
    rows = near.reshape(4, count).astype(jnp.bfloat16)
    rows = jnp.zeros((16, width), jnp.bfloat16).at[:4, :count].set(rows)
    sheet = jnp.concatenate([key_points.reshape(images * n, width), rows])
    place = jnp.stack([g % 4, g // 4, g % 2])
    handler = (pair_second // 4) % 4 ^ (g % 4)
    own_1, own_2, pair, sheet, near, place, handler = lax.optimization_barrier(
        (own_1, own_2, pair, sheet, near, place, handler)
    )

    pair_1 = move(pair, Z_1)
    own_3_pair_2 = move(join(own_2, pair), Z_2)
    k_3 = move(after(k_1, pair), Y_1)
    k_2 = move(after(key_points, pair, k_core), Y_2)
    sheet_far = lax.ppermute(sheet, "grp", X_FAR)
    total = add_blocks(own, (own, own_1, own_2, pair))
    found = match_pairs(place, after(near, total), (key_points, k_core), {0: key_points, 3: k_1})


    pair_3 = move(after(pair_1, found), Z_1)
    total = add_blocks(own, (pair_1,), total)
    far_core = [lax.ppermute(v, "grp", CORE) for v in split(after(sheet_far, found, total), 2)]
    far = sheet_far[images * n:images * n + 4, :count].astype(jnp.int32).reshape(2, 2, count)
    every = jnp.concatenate([near, far])
    found = match_pairs(
        place, every, (key_points, k_core, sheet_far, *far_core),
        {0: key_points, 1: k_2, 2: k_3, 3: k_1}, found, (2, (0, 3)),
    )
    found = found.reshape(4, count, 2, n)
    back = [
        found[0],
        lax.ppermute(found[1], "grp", CORE),
        lax.ppermute(found[2], "grp", X_FAR),
        lax.ppermute(found[3], "grp", X_FAR_CORE),
    ]
    total = add_blocks(own, (own_3_pair_2,), after(total, found))
    expanded = add_blocks(own, (pair_3,), total, last=True)
    handler = after(handler, expanded)[:, None, None]
    confidence = jnp.where(
        handler == 0, back[0], jnp.where(handler == 1, back[1], jnp.where(handler == 2, back[2], back[3]))
    )
    return (expanded, confidence)


def solution(mesh):
    in_specs = (
        P(("grp", "blk"), None),
        P(("grp", "blk"), None, None),
        P(("grp", "blk")),
        P(("grp", "blk")),
    )
    out_specs = (P(("grp", "blk"), None), P(("grp", "blk"), None, None))
    return jax.shard_map(
        on_device, mesh=mesh, in_specs=in_specs, out_specs=out_specs, check_vma=False
    )
```

```python
import functools
import math

import jax
import jax.numpy as jnp
from jax import lax
from jax.experimental import pallas as pl
from jax.experimental.pallas import tpu as pltpu
from jax.sharding import PartitionSpec as P

softmax_sharpness = 10.0
epsilon = 1e-06
log2_e = 1.4426950408889634
vmem_bytes = 12 * 2**20

def steps(axis, turn):
    pairs = []
    for device in range(128):
        blk, grp = device // 16, device % 16
        hop = turn if grp % 2 == 0 else -turn
        if axis == "z":
            blk = blk // 4 * 4 + (blk + hop) % 4
        else:
            grp = (grp // 4 + hop) % 4 * 4 + grp % 4
        pairs.append((device, blk * 16 + grp))
    return pairs


BOTH = ("blk", "grp")
Z_1, Z_2, Y_1, Y_2 = steps("z", 1), steps("z", -1), steps("y", 1), steps("y", -1)
X_PAIR = [(i, i ^ 4) for i in range(8)]
CORE = [(i, i ^ 1) for i in range(16)]
X_FAR = [(i, i ^ 2) for i in range(16)]
X_FAR_CORE = [(i, i ^ 3) for i in range(16)]


def fold_lanes(op, x):
    return op(op(x[:, 0:128], x[:, 128:256]), op(x[:, 256:384], x[:, 384:512]))


def confidences(t, row_lse, col_lse, out_ref, where):
    rows, m = t[0].shape
    half = 0.5 / softmax_sharpness
    offset = 2.0 * math.log(m)
    row_half, col_half = row_lse * half, col_lse * half
    best = jnp.full((8, m), -jnp.inf, jnp.float32)
    row_best = []
    for k, part in enumerate(t):
        part = part[...]
        sl = slice(k * rows, (k + 1) * rows)
        tile = jnp.transpose(jnp.broadcast_to(row_half[:, sl], (128, rows)))
        tile = jnp.concatenate([tile] * (m // 128), axis=1)
        best = jnp.maximum(best, jnp.max((part - tile).reshape(rows // 8, 8, m), axis=0))
        row_best.append(
            jnp.max(jnp.transpose(fold_lanes(jnp.maximum, part - col_half)), axis=0, keepdims=True)
        )
    out_ref[where, 0:1, :] = jnp.concatenate(row_best, axis=1) * (1.0 / half) - row_lse + offset
    out_ref[where, 1:2, :] = jnp.max(best, axis=0, keepdims=True) * (1.0 / half) - col_lse + offset


def match_two(pairs, out_ref):
    rows = 256
    sums = []
    for a_ref, b_ref, t_ref, _ in pairs:
        n, m = t_ref.shape
        col = jnp.zeros((8, m), jnp.float32)
        row_sums = []
        for k in range(n // rows):
            sl = slice(k * rows, (k + 1) * rows)
            t = lax.dot_general(
                a_ref[sl, :], b_ref[...], (((1,), (1,)), ((), ())), preferred_element_type=jnp.float32
            )
            t_ref[sl, :] = t
            e = jnp.exp2(t * (softmax_sharpness * log2_e))
            row_sums.append(jnp.sum(jnp.transpose(fold_lanes(jnp.add, e)), axis=0, keepdims=True))
            col = col + jnp.sum(e.reshape(rows // 8, 8, m), axis=0)
        sums.append((jnp.concatenate(row_sums, axis=1), jnp.sum(col, axis=0, keepdims=True)))
    low = functools.reduce(jnp.minimum, [x for both in sums for x in both])
    high = functools.reduce(jnp.maximum, [x for both in sums for x in both])
    in_range = (jnp.min(low) > 1e-25) & (jnp.max(high) < 1e30)
    for (_, _, t_ref, where), (row_sum, col_sum) in zip(pairs, sums):
        parts = [t_ref.at[k:k + rows, :] for k in range(0, t_ref.shape[0], rows)]
        confidences(parts, jnp.log(row_sum), jnp.log(col_sum), out_ref, where)

    @pl.when(jnp.logical_not(in_range))
    def _():
        for _, _, t_ref, where in pairs:
            n = t_ref.shape[0]
            s = t_ref[...] * softmax_sharpness
            peak = jnp.max(s, axis=0, keepdims=True)
            col_lse = jnp.log(jnp.sum(jnp.exp(s - peak), axis=0, keepdims=True)) + peak
            peak = jnp.max(s, axis=1, keepdims=True)
            row_lse = jnp.log(jnp.sum(jnp.exp(s - peak), axis=1, keepdims=True)) + peak
            row_lse = jnp.transpose(jnp.broadcast_to(row_lse, (n, 128)))[0:1, :]
            parts = [t_ref.at[k:k + rows, :] for k in range(0, n, rows)]
            confidences(parts, row_lse, col_lse, out_ref, where)


def pairs_kernel(place_ref, meta_ref, *rest, owners, steps, skip):
    rest = list(rest)
    firsts = [rest.pop(0) for _ in range(owners)]
    seconds = {step: rest.pop(0) for step in steps}
    before_ref = rest.pop(0) if skip else None
    out_ref, list_ref, a_0, b_0, t_0, a_1, b_1, t_1 = rest
    lists, _, count = meta_ref.shape
    n = t_0.shape[0]
    mine, my_y = place_ref[0], place_ref[1]
    turn = 1 + 2 * place_ref[2]
    if skip:
        out_ref[...] = before_ref[...]

    total = jnp.int32(0)
    for owner in range(lists):
        for p in range(count):
            second = meta_ref[owner, 1, p]
            source = lax.shift_right_logical(second, 2)
            step = ((lax.shift_right_logical(source, 2) - my_y + 4) * turn) & 3
            hit = (source & 3) == mine
            if skip:
                done_owners, done_steps = skip
                if owner < done_owners:
                    hit = hit & functools.reduce(
                        jnp.logical_and, [step != k for k in done_steps]
                    )
            elif len(steps) < 4:
                hit = hit & functools.reduce(jnp.logical_or, [step == k for k in steps])
            list_ref[total] = (
                (owner + (owner * count + p) * 256) + meta_ref[owner, 0, p] * 4 + step * 16 + (second & 3) * 64
            )
            total = total + hit.astype(jnp.int32)

    def load(i, a_ref, b_ref):
        code = list_ref[jnp.minimum(i, total - 1)]
        owner = code & 3
        image = lax.shift_right_logical(code, 2) & 3
        step = lax.shift_right_logical(code, 4) & 3
        row = lax.shift_right_logical(code, 6) & 3
        rows = pl.ds(pl.multiple_of(image * n, n), n)
        for k, ref in enumerate(firsts[:3]):
            @pl.when(owner == k)
            def _():
                a_ref[...] = ref[image] if len(ref.shape) == 3 else ref[rows, :]
        for k, ref in enumerate(firsts[3:]):
            held = ref.shape[0] // n
            @pl.when((owner == 3) & (image >= k * held) & (image < (k + 1) * held))
            def _():
                inside = pl.multiple_of((image - k * held) * n, n)
                a_ref[...] = ref[pl.ds(inside, n), :]
        for k, ref in seconds.items():
            @pl.when(step == k)
            def _():
                b_ref[...] = ref[row]
        return lax.shift_right_logical(code, 8)

    def two(i, carry):
        where_0 = load(2 * i, a_0, b_0)
        where_1 = load(2 * i + 1, a_1, b_1)
        match_two(((a_0, b_0, t_0, where_0), (a_1, b_1, t_1, where_1)), out_ref)
        return carry

    lax.fori_loop(0, lax.shift_right_logical(total + 1, 1), two, 0)


def match_pairs(place, meta, firsts, seconds, before=None, skip=None):
    _, n, width = seconds[3].shape
    count = meta.shape[2]
    smem = pl.BlockSpec(memory_space=pltpu.SMEM)
    vmem = pl.BlockSpec(memory_space=pltpu.VMEM)
    arrays = (*firsts, *seconds.values()) + (() if before is None else (before,))
    return pl.pallas_call(
        functools.partial(pairs_kernel, owners=len(firsts), steps=tuple(seconds), skip=skip),
        out_shape=jax.ShapeDtypeStruct((4 * count, 2, n), jnp.float32),
        in_specs=[smem, smem] + [vmem] * len(arrays),
        out_specs=vmem,
        scratch_shapes=[
            pltpu.SMEM((4 * count + 1,), jnp.int32),
        ] + 2 * [
            pltpu.VMEM((n, width), jnp.bfloat16),
            pltpu.VMEM((n, width), jnp.bfloat16),
            pltpu.VMEM((n, n), jnp.float32),
        ],
        compiler_params=pltpu.CompilerParams(vmem_limit_bytes=vmem_bytes),
        cost_estimate=pl.CostEstimate(
            flops=n, bytes_accessed=n, transcendentals=0
        ),
        name="match_pairs",
    )(place, meta, *arrays)


def after(x, *deps):
    return lax.optimization_barrier((x,) + deps)[0]


def block_kernel(own_ref, *rest, pieces, first, last):
    rest = list(rest)
    blocks = [rest.pop(0) for _ in range(pieces)]
    total_ref = None if first else rest.pop(0)
    out_ref, weights_ref = rest[:2]
    wide = 256
    n = own_ref.shape[1]
    at = 0
    for block in blocks:
        for q in range(0, block.shape[0], wide):
            sims = lax.dot_general(
                own_ref[...], block[q:q + wide, :], (((1,), (1,)), ((), ())),
                preferred_element_type=jnp.float32,
            )
            weights_ref[:, at:at + wide] = jnp.maximum(sims, 0.0).astype(jnp.bfloat16)
            at += wide
    square = None
    for c in range(0, n, wide):
        total = None if first else total_ref[:, c:c + wide]
        at = 0
        for block in blocks:
            h = block.shape[0]
            part = jnp.dot(
                weights_ref[:, at:at + h], block[:, c:c + wide], preferred_element_type=jnp.float32
            )
            total = part if total is None else total + part
            at += h
        if last:
            total_ref[:, c:c + wide] = total
            folded = total[:, :128] * total[:, :128] + total[:, 128:] * total[:, 128:]
            square = folded if square is None else square + folded
        else:
            out_ref[:, c:c + wide] = total
    if last:
        scale = lax.rsqrt(jnp.sum(square, axis=1, keepdims=True) * (1.0 / n) + epsilon)
        result_ref, sems = rest[2:4]
        rows = own_ref.shape[0] // 4
        copies = []
        for i in range(4):
            sl = slice(i * rows, (i + 1) * rows)
            result_ref[sl, :] = (total_ref[sl, :] * scale[sl, :]).astype(result_ref.dtype)
            copies.append(pltpu.make_async_copy(result_ref.at[sl, :], out_ref.at[sl, :], sems.at[i]))
            copies[-1].start()
        for copy in copies:
            copy.wait()


def add_blocks(own, blocks, total=None, last=False):
    rows, n = own.shape
    count = sum(b.shape[0] for b in blocks)
    vmem = pl.BlockSpec(memory_space=pltpu.VMEM)
    args = (own, *blocks) + (() if total is None else (total,))
    return pl.pallas_call(
        functools.partial(block_kernel, pieces=len(blocks), first=total is None, last=last),
        out_shape=jax.ShapeDtypeStruct((rows, n), jnp.bfloat16 if last else jnp.float32),
        in_specs=[vmem] * len(args),
        out_specs=pl.BlockSpec(memory_space=pl.ANY) if last else vmem,
        scratch_shapes=[pltpu.VMEM((rows, count), jnp.bfloat16)]
        + ([pltpu.VMEM((rows, n), jnp.bfloat16), pltpu.SemaphoreType.DMA((4,))] if last else []),
        compiler_params=pltpu.CompilerParams(vmem_limit_bytes=vmem_bytes),
        cost_estimate=pl.CostEstimate(
            flops=n, bytes_accessed=n, transcendentals=0
        ),
        name="add_blocks",
    )(*args)


def join_kernel(a_ref, b_ref, out_ref):
    out_ref[: a_ref.shape[0], :] = a_ref[...]
    out_ref[a_ref.shape[0]:, :] = b_ref[...]


def join(a, b):
    vmem = pl.BlockSpec(memory_space=pltpu.VMEM)
    return pl.pallas_call(
        join_kernel,
        out_shape=jax.ShapeDtypeStruct((a.shape[0] + b.shape[0], a.shape[1]), a.dtype),
        in_specs=[vmem] * 2,
        out_specs=vmem,
        compiler_params=pltpu.CompilerParams(vmem_limit_bytes=vmem_bytes),
        cost_estimate=pl.CostEstimate(flops=1, bytes_accessed=1, transcendentals=0),
        name="join",
    )(a, b)


def split_kernel(a_ref, *rest):
    outs, sems = rest[:-1], rest[-1]
    rows = outs[0].shape[0]
    copies = [
        pltpu.make_async_copy(a_ref.at[i * rows:(i + 1) * rows], out, sems.at[i])
        for i, out in enumerate(outs)
    ]
    for copy in copies:
        copy.start()
    for copy in copies:
        copy.wait()


def split(a, count):
    hbm = pl.BlockSpec(memory_space=pl.ANY)
    rows, width = a.shape[0] // count // 16 * 16, a.shape[1]
    return pl.pallas_call(
        split_kernel,
        out_shape=[jax.ShapeDtypeStruct((rows, width), a.dtype)] * count,
        in_specs=[hbm],
        out_specs=[hbm] * count,
        scratch_shapes=[pltpu.SemaphoreType.DMA((count,))],
        compiler_params=pltpu.CompilerParams(vmem_limit_bytes=vmem_bytes),
        cost_estimate=pl.CostEstimate(flops=1, bytes_accessed=1, transcendentals=0),
        name="split",
    )(a)


def on_device(global_desc, key_points, pair_first, pair_second):
    g = lax.axis_index("grp")
    images, n, width = key_points.shape
    count = pair_second.shape[0]

    def move(v, perm):
        return lax.ppermute(v, BOTH, perm)

    own = global_desc
    own_1 = move(own, Z_1)
    own_2 = move(own, Z_2)
    pair = lax.ppermute(own, "blk", X_PAIR)
    k_core = lax.ppermute(key_points, "grp", CORE)
    k_1 = move(key_points, Y_1)
    lists = jnp.stack([pair_first, pair_second])
    near = jnp.stack([lists, lax.ppermute(lists, "grp", CORE)])
    rows = near.reshape(4, count).astype(jnp.bfloat16)
    rows = jnp.zeros((16, width), jnp.bfloat16).at[:4, :count].set(rows)
    sheet = jnp.concatenate([key_points.reshape(images * n, width), rows])
    place = jnp.stack([g % 4, g // 4, g % 2])
    handler = (pair_second // 4) % 4 ^ (g % 4)
    own_1, own_2, pair, sheet, near, place, handler = lax.optimization_barrier(
        (own_1, own_2, pair, sheet, near, place, handler)
    )

    pair_1 = move(pair, Z_1)
    own_3_pair_2 = move(join(own_2, pair), Z_2)
    k_3 = move(after(k_1, pair), Y_1)
    k_2 = move(after(key_points, pair, k_core), Y_2)
    sheet_far = lax.ppermute(sheet, "grp", X_FAR)
    total = add_blocks(own, (own, own_1, own_2, pair))
    found = match_pairs(place, after(near, total), (key_points, k_core), {0: key_points, 3: k_1})


    pair_3 = move(after(pair_1, found), Z_1)
    total = add_blocks(own, (pair_1,), total)
    far_core = [lax.ppermute(v, "grp", CORE) for v in split(after(sheet_far, found, total), 2)]
    far = sheet_far[images * n:images * n + 4, :count].astype(jnp.int32).reshape(2, 2, count)
    every = jnp.concatenate([near, far])
    found = match_pairs(
        place, every, (key_points, k_core, sheet_far, *far_core),
        {0: key_points, 1: k_2, 2: k_3, 3: k_1}, found, (2, (0, 3)),
    )
    found = found.reshape(4, count, 2, n)
    back = [
        found[0],
        lax.ppermute(found[1], "grp", CORE),
        lax.ppermute(found[2], "grp", X_FAR),
        lax.ppermute(found[3], "grp", X_FAR_CORE),
    ]
    total = add_blocks(own, (own_3_pair_2,), after(total, found))
    expanded = add_blocks(own, (pair_3,), total, last=True)
    handler = after(handler, expanded)[:, None, None]
    confidence = jnp.where(
        handler == 0, back[0], jnp.where(handler == 1, back[1], jnp.where(handler == 2, back[2], back[3]))
    )
    return (expanded, confidence)


def solution(mesh):
    in_specs = (
        P(("grp", "blk"), None),
        P(("grp", "blk"), None, None),
        P(("grp", "blk")),
        P(("grp", "blk")),
    )
    out_specs = (P(("grp", "blk"), None), P(("grp", "blk"), None, None))
    return jax.shard_map(
        on_device, mesh=mesh, in_specs=in_specs, out_specs=out_specs, check_vma=False
    )
```

```python
import functools
import math

import jax
import jax.numpy as jnp
from jax import lax
from jax.experimental import pallas as pl
from jax.experimental.pallas import tpu as pltpu
from jax.sharding import PartitionSpec as P

softmax_sharpness = 10.0
epsilon = 1e-06
log2_e = 1.4426950408889634
vmem_bytes = 12 * 2**20

def steps(axis, turn):
    pairs = []
    for device in range(128):
        blk, grp = device // 16, device % 16
        hop = turn if grp % 2 == 0 else -turn
        if axis == "z":
            blk = blk // 4 * 4 + (blk + hop) % 4
        else:
            grp = (grp // 4 + hop) % 4 * 4 + grp % 4
        pairs.append((device, blk * 16 + grp))
    return pairs


BOTH = ("blk", "grp")
Z_1, Z_2, Y_1, Y_2 = steps("z", 1), steps("z", -1), steps("y", 1), steps("y", -1)
X_PAIR = [(i, i ^ 4) for i in range(8)]
CORE = [(i, i ^ 1) for i in range(16)]
X_FAR = [(i, i ^ 2) for i in range(16)]
X_FAR_CORE = [(i, i ^ 3) for i in range(16)]


def fold_lanes(op, x):
    return op(op(x[:, 0:128], x[:, 128:256]), op(x[:, 256:384], x[:, 384:512]))


def confidences(t, row_lse, col_lse, out_ref, where):
    rows, m = t[0].shape
    half = 0.5 / softmax_sharpness
    offset = 2.0 * math.log(m)
    row_half, col_half = row_lse * half, col_lse * half
    best = jnp.full((8, m), -jnp.inf, jnp.float32)
    row_best = []
    for k, part in enumerate(t):
        part = part[...]
        sl = slice(k * rows, (k + 1) * rows)
        tile = jnp.transpose(jnp.broadcast_to(row_half[:, sl], (128, rows)))
        tile = jnp.concatenate([tile] * (m // 128), axis=1)
        best = jnp.maximum(best, jnp.max((part - tile).reshape(rows // 8, 8, m), axis=0))
        row_best.append(
            jnp.max(jnp.transpose(fold_lanes(jnp.maximum, part - col_half)), axis=0, keepdims=True)
        )
    out_ref[where, 0:1, :] = jnp.concatenate(row_best, axis=1) * (1.0 / half) - row_lse + offset
    out_ref[where, 1:2, :] = jnp.max(best, axis=0, keepdims=True) * (1.0 / half) - col_lse + offset


def match_two(pairs, out_ref):
    rows = 256
    sums = []
    for a_ref, b_ref, t_ref, _ in pairs:
        n, m = t_ref.shape
        col = jnp.zeros((8, m), jnp.float32)
        row_sums = []
        for k in range(n // rows):
            sl = slice(k * rows, (k + 1) * rows)
            t = lax.dot_general(
                a_ref[sl, :], b_ref[...], (((1,), (1,)), ((), ())), preferred_element_type=jnp.float32
            )
            t_ref[sl, :] = t
            e = jnp.exp2(t * (softmax_sharpness * log2_e))
            row_sums.append(jnp.sum(jnp.transpose(fold_lanes(jnp.add, e)), axis=0, keepdims=True))
            col = col + jnp.sum(e.reshape(rows // 8, 8, m), axis=0)
        sums.append((jnp.concatenate(row_sums, axis=1), jnp.sum(col, axis=0, keepdims=True)))
    low = functools.reduce(jnp.minimum, [x for both in sums for x in both])
    high = functools.reduce(jnp.maximum, [x for both in sums for x in both])
    in_range = (jnp.min(low) > 1e-25) & (jnp.max(high) < 1e30)
    for (_, _, t_ref, where), (row_sum, col_sum) in zip(pairs, sums):
        parts = [t_ref.at[k:k + rows, :] for k in range(0, t_ref.shape[0], rows)]
        confidences(parts, jnp.log(row_sum), jnp.log(col_sum), out_ref, where)

    @pl.when(jnp.logical_not(in_range))
    def _():
        for _, _, t_ref, where in pairs:
            n = t_ref.shape[0]
            s = t_ref[...] * softmax_sharpness
            peak = jnp.max(s, axis=0, keepdims=True)
            col_lse = jnp.log(jnp.sum(jnp.exp(s - peak), axis=0, keepdims=True)) + peak
            peak = jnp.max(s, axis=1, keepdims=True)
            row_lse = jnp.log(jnp.sum(jnp.exp(s - peak), axis=1, keepdims=True)) + peak
            row_lse = jnp.transpose(jnp.broadcast_to(row_lse, (n, 128)))[0:1, :]
            parts = [t_ref.at[k:k + rows, :] for k in range(0, n, rows)]
            confidences(parts, row_lse, col_lse, out_ref, where)


def pairs_kernel(place_ref, meta_ref, *rest, owners, steps, skip):
    rest = list(rest)
    firsts = [rest.pop(0) for _ in range(owners)]
    seconds = {step: rest.pop(0) for step in steps}
    before_ref = rest.pop(0) if skip else None
    out_ref, list_ref, a_0, b_0, t_0, a_1, b_1, t_1 = rest
    lists, _, count = meta_ref.shape
    n = t_0.shape[0]
    mine, my_y = place_ref[0], place_ref[1]
    turn = 1 + 2 * place_ref[2]
    if skip:
        out_ref[...] = before_ref[...]

    total = jnp.int32(0)
    for owner in range(lists):
        for p in range(count):
            second = meta_ref[owner, 1, p]
            source = lax.shift_right_logical(second, 2)
            step = ((lax.shift_right_logical(source, 2) - my_y + 4) * turn) & 3
            hit = (source & 3) == mine
            if skip:
                done_owners, done_steps = skip
                if owner < done_owners:
                    hit = hit & functools.reduce(
                        jnp.logical_and, [step != k for k in done_steps]
                    )
            elif len(steps) < 4:
                hit = hit & functools.reduce(jnp.logical_or, [step == k for k in steps])
            list_ref[total] = (
                (owner + (owner * count + p) * 256) + meta_ref[owner, 0, p] * 4 + step * 16 + (second & 3) * 64
            )
            total = total + hit.astype(jnp.int32)

    def load(i, a_ref, b_ref):
        code = list_ref[jnp.minimum(i, total - 1)]
        owner = code & 3
        image = lax.shift_right_logical(code, 2) & 3
        step = lax.shift_right_logical(code, 4) & 3
        row = lax.shift_right_logical(code, 6) & 3
        rows = pl.ds(pl.multiple_of(image * n, n), n)
        for k, ref in enumerate(firsts[:3]):
            @pl.when(owner == k)
            def _():
                a_ref[...] = ref[image] if len(ref.shape) == 3 else ref[rows, :]
        for k, ref in enumerate(firsts[3:]):
            held = ref.shape[0] // n
            @pl.when((owner == 3) & (image >= k * held) & (image < (k + 1) * held))
            def _():
                inside = pl.multiple_of((image - k * held) * n, n)
                a_ref[...] = ref[pl.ds(inside, n), :]
        for k, ref in seconds.items():
            @pl.when(step == k)
            def _():
                b_ref[...] = ref[row]
        return lax.shift_right_logical(code, 8)

    def last():
        where = load(total - 1, a_0, b_0)
        match_two(((a_0, b_0, t_0, where),), out_ref)

    def two(i, carry):
        where_0 = load(2 * i, a_0, b_0)
        where_1 = load(2 * i + 1, a_1, b_1)
        match_two(((a_0, b_0, t_0, where_0), (a_1, b_1, t_1, where_1)), out_ref)
        return carry

    lax.fori_loop(0, lax.shift_right_logical(total, 1), two, 0)
    pl.when((total & 1) == 1)(last)


def match_pairs(place, meta, firsts, seconds, before=None, skip=None):
    _, n, width = seconds[3].shape
    count = meta.shape[2]
    smem = pl.BlockSpec(memory_space=pltpu.SMEM)
    vmem = pl.BlockSpec(memory_space=pltpu.VMEM)
    arrays = (*firsts, *seconds.values()) + (() if before is None else (before,))
    return pl.pallas_call(
        functools.partial(pairs_kernel, owners=len(firsts), steps=tuple(seconds), skip=skip),
        out_shape=jax.ShapeDtypeStruct((4 * count, 2, n), jnp.float32),
        in_specs=[smem, smem] + [vmem] * len(arrays),
        out_specs=vmem,
        scratch_shapes=[
            pltpu.SMEM((4 * count + 1,), jnp.int32),
        ] + 2 * [
            pltpu.VMEM((n, width), jnp.bfloat16),
            pltpu.VMEM((n, width), jnp.bfloat16),
            pltpu.VMEM((n, n), jnp.float32),
        ],
        compiler_params=pltpu.CompilerParams(vmem_limit_bytes=vmem_bytes),
        cost_estimate=pl.CostEstimate(
            flops=n, bytes_accessed=n, transcendentals=0
        ),
        name="match_pairs",
    )(place, meta, *arrays)


def after(x, *deps):
    return lax.optimization_barrier((x,) + deps)[0]


def block_kernel(own_ref, *rest, pieces, first, last):
    rest = list(rest)
    blocks = [rest.pop(0) for _ in range(pieces)]
    total_ref = None if first else rest.pop(0)
    out_ref, weights_ref = rest[:2]
    wide = 256
    n = own_ref.shape[1]
    at = 0
    for block in blocks:
        for q in range(0, block.shape[0], wide):
            sims = lax.dot_general(
                own_ref[...], block[q:q + wide, :], (((1,), (1,)), ((), ())),
                preferred_element_type=jnp.float32,
            )
            weights_ref[:, at:at + wide] = jnp.maximum(sims, 0.0).astype(jnp.bfloat16)
            at += wide
    square = None
    for c in range(0, n, wide):
        total = None if first else total_ref[:, c:c + wide]
        at = 0
        for block in blocks:
            h = block.shape[0]
            part = jnp.dot(
                weights_ref[:, at:at + h], block[:, c:c + wide], preferred_element_type=jnp.float32
            )
            total = part if total is None else total + part
            at += h
        if last:
            total_ref[:, c:c + wide] = total
            folded = total[:, :128] * total[:, :128] + total[:, 128:] * total[:, 128:]
            square = folded if square is None else square + folded
        else:
            out_ref[:, c:c + wide] = total
    if last:
        scale = lax.rsqrt(jnp.sum(square, axis=1, keepdims=True) * (1.0 / n) + epsilon)
        for c in range(0, n, wide):
            out_ref[:, c:c + wide] = (total_ref[:, c:c + wide] * scale).astype(out_ref.dtype)


def add_blocks(own, blocks, total=None, last=False):
    rows, n = own.shape
    count = sum(b.shape[0] for b in blocks)
    vmem = pl.BlockSpec(memory_space=pltpu.VMEM)
    args = (own, *blocks) + (() if total is None else (total,))
    return pl.pallas_call(
        functools.partial(block_kernel, pieces=len(blocks), first=total is None, last=last),
        out_shape=jax.ShapeDtypeStruct((rows, n), jnp.bfloat16 if last else jnp.float32),
        in_specs=[vmem] * len(args),
        out_specs=vmem,
        scratch_shapes=[pltpu.VMEM((rows, count), jnp.bfloat16)],
        compiler_params=pltpu.CompilerParams(vmem_limit_bytes=vmem_bytes),
        cost_estimate=pl.CostEstimate(
            flops=n, bytes_accessed=n, transcendentals=0
        ),
        name="add_blocks",
    )(*args)


def join_kernel(a_ref, b_ref, out_ref):
    out_ref[: a_ref.shape[0], :] = a_ref[...]
    out_ref[a_ref.shape[0]:, :] = b_ref[...]


def join(a, b):
    vmem = pl.BlockSpec(memory_space=pltpu.VMEM)
    return pl.pallas_call(
        join_kernel,
        out_shape=jax.ShapeDtypeStruct((a.shape[0] + b.shape[0], a.shape[1]), a.dtype),
        in_specs=[vmem] * 2,
        out_specs=vmem,
        compiler_params=pltpu.CompilerParams(vmem_limit_bytes=vmem_bytes),
        cost_estimate=pl.CostEstimate(flops=1, bytes_accessed=1, transcendentals=0),
        name="join",
    )(a, b)


def split_kernel(a_ref, *rest):
    outs, sems = rest[:-1], rest[-1]
    rows = outs[0].shape[0]
    copies = [
        pltpu.make_async_copy(a_ref.at[i * rows:(i + 1) * rows], out, sems.at[i])
        for i, out in enumerate(outs)
    ]
    for copy in copies:
        copy.start()
    for copy in copies:
        copy.wait()


def split(a, count):
    hbm = pl.BlockSpec(memory_space=pl.ANY)
    rows, width = a.shape[0] // count // 16 * 16, a.shape[1]
    return pl.pallas_call(
        split_kernel,
        out_shape=[jax.ShapeDtypeStruct((rows, width), a.dtype)] * count,
        in_specs=[hbm],
        out_specs=[hbm] * count,
        scratch_shapes=[pltpu.SemaphoreType.DMA((count,))],
        compiler_params=pltpu.CompilerParams(vmem_limit_bytes=vmem_bytes),
        cost_estimate=pl.CostEstimate(flops=1, bytes_accessed=1, transcendentals=0),
        name="split",
    )(a)


def on_device(global_desc, key_points, pair_first, pair_second):
    g = lax.axis_index("grp")
    images, n, width = key_points.shape
    count = pair_second.shape[0]

    def move(v, perm):
        return lax.ppermute(v, BOTH, perm)

    own = global_desc
    own_1 = move(own, Z_1)
    own_2 = move(own, Z_2)
    pair = lax.ppermute(own, "blk", X_PAIR)
    k_core = lax.ppermute(key_points, "grp", CORE)
    k_1 = move(key_points, Y_1)
    lists = jnp.stack([pair_first, pair_second])
    near = jnp.stack([lists, lax.ppermute(lists, "grp", CORE)])
    rows = near.reshape(4, count).astype(jnp.bfloat16)
    rows = jnp.zeros((16, width), jnp.bfloat16).at[:4, :count].set(rows)
    sheet = jnp.concatenate([key_points.reshape(images * n, width), rows])
    place = jnp.stack([g % 4, g // 4, g % 2])
    handler = (pair_second // 4) % 4 ^ (g % 4)
    own_1, own_2, pair, sheet, near, place, handler = lax.optimization_barrier(
        (own_1, own_2, pair, sheet, near, place, handler)
    )

    pair_1 = move(pair, Z_1)
    own_3_pair_2 = move(join(own_2, pair), Z_2)
    k_3 = move(after(k_1, pair), Y_1)
    k_2 = move(after(key_points, pair, k_core), Y_2)
    sheet_far = lax.ppermute(sheet, "grp", X_FAR)
    total = add_blocks(own, (own, own_1, own_2, pair))
    found = match_pairs(place, after(near, total), (key_points, k_core), {0: key_points, 3: k_1})


    pair_3 = move(after(pair_1, found), Z_1)
    total = add_blocks(own, (pair_1,), total)
    far_core = [lax.ppermute(v, "grp", CORE) for v in split(after(sheet_far, found, total), 2)]
    far = sheet_far[images * n:images * n + 4, :count].astype(jnp.int32).reshape(2, 2, count)
    every = jnp.concatenate([near, far])
    found = match_pairs(
        place, every, (key_points, k_core, sheet_far, *far_core),
        {0: key_points, 1: k_2, 2: k_3, 3: k_1}, found, (2, (0, 3)),
    )
    found = found.reshape(4, count, 2, n)
    back = [
        found[0],
        lax.ppermute(found[1], "grp", CORE),
        lax.ppermute(found[2], "grp", X_FAR),
        lax.ppermute(found[3], "grp", X_FAR_CORE),
    ]
    total = add_blocks(own, (own_3_pair_2,), after(total, found))
    expanded = add_blocks(own, (pair_3,), total, last=True)
    handler = after(handler, expanded)[:, None, None]
    confidence = jnp.where(
        handler == 0, back[0], jnp.where(handler == 1, back[1], jnp.where(handler == 2, back[2], back[3]))
    )
    return (expanded, confidence)


def solution(mesh):
    in_specs = (
        P(("grp", "blk"), None),
        P(("grp", "blk"), None, None),
        P(("grp", "blk")),
        P(("grp", "blk")),
    )
    out_specs = (P(("grp", "blk"), None), P(("grp", "blk"), None, None))
    return jax.shard_map(
        on_device, mesh=mesh, in_specs=in_specs, out_specs=out_specs, check_vma=False
    )
```
